32 devices in a mesh: seq: 8 (over z, y), head: 4 (over x, core).
Axes of the slice: x: 2, y: 2, z: 4, core: 2. Of those that a mesh axis runs over, the one named last changes fastest.
Arguments:
- hidden_in: bfloat16 [2, 4096, 1024], P(None, 'seq'), may hold values from -6 to 6
- norm_gain: bfloat16 [1024], replicated, may hold values from 0.099609375 to 1.8984375
- query_weight: bfloat16 [1024, 512], P(None, 'head'), may hold values from -0.1875 to 0.1875
- keyvalue_matrix: bfloat16 [1024, 2, 128], replicated, may hold values from -0.1875 to 0.1875
- output_weight: bfloat16 [512, 1024], P('head'), may hold values from -2 to 2
- zgate_weight: bfloat16 [1024, 1536], P(None, 'head'), may hold values from -0.1875 to 0.1875
- inner_weight: bfloat16 [1024, 1536], P(None, 'head'), may hold values from -0.1875 to 0.1875
- state_weight: bfloat16 [1024, 256], replicated, may hold values from -0.1875 to 0.1875
- step_weight: bfloat16 [1024, 24], P(None, 'head'), may hold values from -0.5 to 0.5
- conv_inner: bfloat16 [4, 1536], P(None, 'head'), may hold values from -3 to 3
- conv_state: bfloat16 [4, 256], replicated, may hold values from -3 to 3
- step_bias: float32 [24], P('head'), may hold values from -4 to 0.5
- decay_log: float32 [24], P('head'), may hold values from -4.5 to 0.5
- skip_gain: float32 [24], P('head'), may hold values from 0.5 to 4
- ssm_gain: bfloat16 [1536], P('head'), may hold values from 0.099609375 to 1.8984375
- mixer_weight: bfloat16 [1536, 1024], P('head'), may hold values from -0.15625 to 0.15625
- mlp_gain: bfloat16 [1024], replicated, may hold values from 0.099609375 to 1.8984375
- gate_weight: bfloat16 [1024, 2048], P(None, 'head'), may hold values from -0.1875 to 0.1875
- up_weight: bfloat16 [1024, 2048], P(None, 'head'), may hold values from -0.1875 to 0.1875
- down_weight: bfloat16 [2048, 1024], P('head'), may hold values from -0.125 to 0.125
- grad_output: bfloat16 [2, 4096, 1024], P(None, 'seq'), may hold values from -6 to 6
Outputs:
- output: bfloat16 [2, 4096, 1024], P(None, 'seq')
- grad_input: float32 [2, 4096, 1024], P(None, 'seq')
- grad_norm_gain: float32 [1024], replicated
- grad_query_weight: float32 [1024, 512], P(None, 'head')
- grad_keyvalue_weight: float32 [1024, 2, 128], replicated
- grad_output_weight: float32 [512, 1024], P('head')
- grad_zgate_weight: float32 [1024, 1536], P(None, 'head')
- grad_inner_weight: float32 [1024, 1536], P(None, 'head')
- grad_state_weight: float32 [1024, 256], replicated
- grad_step_weight: float32 [1024, 24], P(None, 'head')
- grad_conv_inner: float32 [4, 1536], P(None, 'head')
- grad_conv_state: float32 [4, 256], replicated
- grad_step_bias: float32 [24], P('head')
- grad_decay_log: float32 [24], P('head')
- grad_skip_gain: float32 [24], P('head')
- grad_ssm_gain: float32 [1536], P('head')
- grad_mixer_weight: float32 [1536, 1024], P('head')
- grad_mlp_gain: float32 [1024], replicated
- grad_gate_weight: float32 [1024, 2048], P(None, 'head')
- grad_up_weight: float32 [1024, 2048], P(None, 'head')
- grad_down_weight: float32 [2048, 1024], P('head')
The draws below stay inside these ranges and needn't reach their ends.
All inputs are finite; a program needn't handle non-finite values.
Results may differ from the reference program's by a relative error of at most 0.013.
The reference program's roundings to bfloat16 on the way count: a program that leaves them out, or rounds other values in their place, can miss the bound.
Values may be sent and summed in bfloat16 or wider, within the bound.
A program may use at most 256 MiB of HBM per device.

```python
import math
import jax
import jax.numpy as jnp
from jax import lax

D = 1024
HEADS = 8
KV_HEADS = 2
HEAD_DIM = 64
MHEADS = 24
MHEAD_DIM = 64
STATE = 128
FF = 2048
CONV = 4
SEQS = 2
SSM = 1536
LENGTH = 4096


def levels(stream_key, extent, shards, low, high):
    factor_of = 1.0
    for position, shards_of in shards:
        draws = jax.random.uniform(jax.random.fold_in(jax.random.fold_in(stream_key, 6), position), (shards_of,), jnp.float32, low / len(shards), high / len(shards))
        factor_of = factor_of * jnp.repeat(jnp.exp(draws), extent[position] // shards_of).reshape((-1,) + (1,) * (len(extent) - 1 - position))
    return factor_of


def noise(stream_key, extent, scale, most, cuts=(), kind=jnp.bfloat16):
    values = scale * jax.random.normal(stream_key, extent, jnp.float32)
    if cuts:
        values = values * levels(stream_key, extent, cuts, -0.22, 0.18)
    return jnp.clip(values, -most, most).astype(kind)


def setup_inputs(seed: int = 0) -> dict:
    arg_keys = jax.random.split(jax.random.key(seed), 22)
    return {
        "hidden_in": noise(arg_keys[0], (SEQS, LENGTH, D), 1.0, 6.0, ((1, 8),)),
        "norm_gain": jnp.clip(1.0 + 0.18 * jax.random.normal(arg_keys[1], (D,), jnp.float32), 0.099609375, 1.8984375).astype(jnp.bfloat16),
        "query_weight": noise(arg_keys[2], (D, HEADS * HEAD_DIM), D ** -0.5, 0.1875, ((1, 4),)),
        "keyvalue_matrix": noise(arg_keys[3], (D, KV_HEADS, 2 * HEAD_DIM), D ** -0.5, 0.1875),
        "output_weight": noise(arg_keys[4], (HEADS * HEAD_DIM, D), 8 ** -0.5, 2.0, ((0, 4),)),
        "zgate_weight": noise(arg_keys[5], (D, SSM), D ** -0.5, 0.1875, ((1, 4),)),
        "inner_weight": noise(arg_keys[6], (D, SSM), D ** -0.5, 0.1875, ((1, 4),)),
        "state_weight": noise(arg_keys[7], (D, 2 * STATE), D ** -0.5, 0.1875),
        "step_weight": noise(arg_keys[8], (D, MHEADS), (D // 8) ** -0.5, 0.5, ((1, 4),)),
        "conv_inner": noise(arg_keys[9], (CONV, SSM), CONV ** -0.5, 3.0, ((1, 4),)),
        "conv_state": noise(arg_keys[10], (CONV, 2 * STATE), CONV ** -0.5, 3.0),
        "step_bias": jnp.clip(-4.0 + 4.5 * jax.random.uniform(arg_keys[11], (MHEADS,), jnp.float32) ** levels(arg_keys[11], (MHEADS,), ((0, 4),), -0.2, 0.2), -4.0, 0.5),
        "decay_log": jnp.clip(-4.5 + 5.0 * jax.random.uniform(arg_keys[12], (MHEADS,), jnp.float32) ** levels(arg_keys[12], (MHEADS,), ((0, 4),), -0.2, 0.2), -4.5, 0.5),
        "skip_gain": jnp.clip(0.5 + 3.5 * jax.random.uniform(arg_keys[13], (MHEADS,), jnp.float32) ** levels(arg_keys[13], (MHEADS,), ((0, 4),), -0.2, 0.2), 0.5, 4.0),
        "ssm_gain": jnp.clip(1.0 + 0.18 * jax.random.normal(arg_keys[14], (SSM,), jnp.float32), 0.099609375, 1.8984375).astype(jnp.bfloat16),
        "mixer_weight": noise(arg_keys[15], (SSM, D), SSM ** -0.5, 0.15625, ((0, 4),)),
        "mlp_gain": jnp.clip(1.0 + 0.18 * jax.random.normal(arg_keys[16], (D,), jnp.float32), 0.099609375, 1.8984375).astype(jnp.bfloat16),
        "gate_weight": noise(arg_keys[17], (D, FF), D ** -0.5, 0.1875, ((1, 4),)),
        "up_weight": noise(arg_keys[18], (D, FF), D ** -0.5, 0.1875, ((1, 4),)),
        "down_weight": noise(arg_keys[19], (FF, D), FF ** -0.5, 0.125, ((0, 4),)),
        "grad_output": noise(arg_keys[20], (SEQS, LENGTH, D), 1.0, 6.0, ((1, 8),)),
    }


@jax.custom_vjp
def low(v):
    return lax.optimization_barrier(v.astype(jnp.bfloat16)).astype(jnp.float32)

@jax.custom_vjp
def low_back(v):
    return v

def low_keep(v):
    return (low(v), None)

def low_pass(kept, grad):
    return (grad,)

def back_keep(v):
    return (v, None)

def back_low(kept, grad):
    return (low(grad),)
low.defvjp(low_keep, low_pass)
low_back.defvjp(back_keep, back_low)
HIGH_ACCURACY = lax.Precision.HIGHEST
EPSILON = 1e-05
ROPE_BASE = 100000000000.0
MASKED = -1e+30

def rms_norm(values, gain):
    factor = lax.rsqrt(lax.optimization_barrier(jnp.mean(values * values, axis=-1, keepdims=True)) + EPSILON)
    return values * factor * gain

def project(left_operand, right_operand):
    return jnp.einsum('uog,gr->uor', left_operand, right_operand, precision=HIGH_ACCURACY)

def rotate(values, positions):
    half = values.shape[-1] // 2
    freq = ROPE_BASE ** (-jnp.arange(half, dtype=jnp.float32) * 2.0 / values.shape[-1])
    angle = positions[:, None] * freq[None, :]
    cosine = jnp.cos(angle)[None, :, None, :]
    sine = jnp.sin(angle)[None, :, None, :]
    first = values[..., :half]
    second = values[..., half:]
    return jnp.concatenate([first * cosine - second * sine, second * cosine + first * sine], axis=-1)

def conv_act(extended, conv_weight):
    rows = extended.shape[1] - (conv_weight.shape[0] - 1)
    summed = extended[:, 0:rows] * conv_weight[0]
    for tap in range(1, conv_weight.shape[0]):
        summed = summed + extended[:, tap:tap + rows] * conv_weight[tap]
    return jax.nn.silu(summed)

def ssm_inputs(extended, step_raw, conv_weight, step_bias, decay_log):
    activated = conv_act(extended, conv_weight)
    inner_width = activated.shape[-1] - 2 * STATE
    heads_here = step_raw.shape[-1]
    channels = activated[..., :inner_width].reshape(activated.shape[0], activated.shape[1], heads_here, inner_width // heads_here)
    writes = activated[..., inner_width:inner_width + STATE]
    reads = activated[..., inner_width + STATE:]
    step = jax.nn.softplus(step_raw + step_bias)
    logdecay = -step * jnp.exp(decay_log)
    return (channels, writes, reads, step, logdecay)

def intra(channels, writes, reads, step, running):
    rows = running.shape[1]
    lower = jnp.arange(rows, dtype=jnp.int32)[:, None] >= jnp.arange(rows, dtype=jnp.int32)[None, :]
    mask = lower[None, :, :, None]
    spread = running[:, :, None, :] - running[:, None, :, :]
    decay = jnp.where(mask, jnp.exp(jnp.where(mask, spread, 0.0)), 0.0)
    intersection = jnp.einsum('stn,sun->stu', reads, writes, precision=HIGH_ACCURACY)
    mixing = decay * intersection[..., None] * step[:, None, :, :]
    within = jnp.einsum('stuh,suhp->sthp', mixing, channels, precision=HIGH_ACCURACY)
    tail_weight = jnp.exp(running[:, -1:, :] - running) * step
    local = jnp.einsum('suh,suhp,sun->shpn', tail_weight, channels, writes, precision=HIGH_ACCURACY)
    return (within, local)

def inter(reads, running, state):
    return jnp.exp(running)[..., None] * jnp.einsum('stn,shpn->sthp', reads, state, precision=HIGH_ACCURACY)

def ssd_block(state, pieces):
    channels, writes, reads, step, logdecay = pieces
    running = jnp.cumsum(logdecay, axis=1)
    within, local = intra(channels, writes, reads, step, running)
    result = within + inter(reads, running, state)
    return (jnp.exp(running[:, -1])[:, :, None, None] * state + local, result)

def attention(queries, keys, values):
    seqs, length, heads, head_dim = queries.shape
    group = heads // keys.shape[2]
    keys_all = jnp.repeat(keys, group, axis=2)
    values_all = jnp.repeat(values, group, axis=2)
    query_block = math.gcd(length, 512)
    factor = head_dim ** (-0.5)
    key_pos = jnp.arange(length, dtype=jnp.int32)

    def one_block(start):
        block_q = lax.dynamic_slice_in_dim(queries, start, query_block, 1)
        scores = jnp.einsum('sqhd,skhd->shqk', block_q, keys_all, precision=HIGH_ACCURACY) * factor
        scores = low_back(scores)
        query_pos = start + jnp.arange(query_block, dtype=jnp.int32)
        allowed = key_pos[None, :] <= query_pos[:, None]
        scores = jnp.where(allowed[None, None], scores, MASKED)
        peak = lax.optimization_barrier(jnp.max(scores, axis=-1, keepdims=True))
        log_total = peak + jnp.log(lax.optimization_barrier(jnp.sum(jnp.exp(scores - peak), axis=-1, keepdims=True)))
        probs = low(jnp.exp(scores - log_total))
        return jnp.einsum('shqk,skhd->sqhd', probs, values_all, precision=HIGH_ACCURACY)
    starts = jnp.arange(length // query_block, dtype=jnp.int32) * query_block
    blocks = lax.map(jax.checkpoint(one_block), starts)
    return jnp.moveaxis(blocks, 0, 1).reshape(seqs, length, heads, head_dim)

def layer(hidden_in, norm_gain, query_weight, keyvalue_matrix, output_weight, zgate_weight, inner_weight, state_weight, step_weight, conv_inner, conv_state, step_bias, decay_log, skip_gain, ssm_gain, mixer_weight, mlp_gain, gate_weight, up_weight, down_weight):
    positions = jnp.arange(LENGTH, dtype=jnp.int32).astype(jnp.float32)
    normalized_input = low(rms_norm(hidden_in, norm_gain))
    query_raw = low_back(project(normalized_input, query_weight)).reshape(SEQS, LENGTH, HEADS, HEAD_DIM)
    queries = low(rotate(query_raw, positions))
    keyvalue_projected = low_back(jnp.einsum('cpf,fky->cpky', normalized_input, keyvalue_matrix, precision=HIGH_ACCURACY))
    keys = low(rotate(keyvalue_projected[..., :HEAD_DIM], positions))
    values = low(keyvalue_projected[..., HEAD_DIM:])
    attended = low_back(low(attention(queries, keys, values))).reshape(SEQS, LENGTH, HEADS * HEAD_DIM)
    zgate = low_back(project(normalized_input, zgate_weight))
    inner = low_back(jnp.concatenate([project(normalized_input, inner_weight), project(normalized_input, state_weight)], axis=-1))
    step_raw = low_back(project(normalized_input, step_weight))
    conv_weight = jnp.concatenate([conv_inner, conv_state], axis=1)
    extended = jnp.pad(inner, ((0, 0), (CONV - 1, 0), (0, 0)))
    channels, writes, reads, step, logdecay = ssm_inputs(extended, step_raw, conv_weight, step_bias, decay_log)
    block_len = math.gcd(LENGTH, 512)
    count = LENGTH // block_len

    def split(values_in):
        return jnp.moveaxis(values_in.reshape((SEQS, count, block_len) + values_in.shape[2:]), 1, 0)
    start_state = jnp.zeros((SEQS, MHEADS, MHEAD_DIM, STATE), jnp.float32)
    pieces = (split(channels), split(writes), split(reads), split(step), split(logdecay))
    final_state, y_blocks = lax.scan(jax.checkpoint(ssd_block), start_state, pieces)
    y_ssm = jnp.moveaxis(y_blocks, 0, 1).reshape(SEQS, LENGTH, MHEADS, MHEAD_DIM) + skip_gain[:, None] * channels
    gated = y_ssm.reshape(SEQS, LENGTH, SSM) * jax.nn.silu(zgate)
    ssm_normed = low(rms_norm(gated, ssm_gain))
    mixed = low_back(project(attended, output_weight) + project(ssm_normed, mixer_weight))
    hidden = hidden_in + mixed
    normed_two = low(rms_norm(hidden, mlp_gain))
    gate = low_back(project(normed_two, gate_weight))
    up = low_back(project(normed_two, up_weight))
    activated = low(jax.nn.silu(gate) * up)
    return hidden + project(activated, down_weight)

def reference(hidden_in, norm_gain, query_weight, keyvalue_matrix, output_weight, zgate_weight, inner_weight, state_weight, step_weight, conv_inner, conv_state, step_bias, decay_log, skip_gain, ssm_gain, mixer_weight, mlp_gain, gate_weight, up_weight, down_weight, grad_output):
    inputs = (hidden_in, norm_gain, query_weight, keyvalue_matrix, output_weight, zgate_weight, inner_weight, state_weight, step_weight, conv_inner, conv_state, step_bias, decay_log, skip_gain, ssm_gain, mixer_weight, mlp_gain, gate_weight, up_weight, down_weight)
    floats = [entry.astype(jnp.float32) for entry in inputs]
    result, pull = jax.vjp(layer, *floats)
    grads = pull(grad_output.astype(jnp.float32))
    return (result.astype(jnp.bfloat16), grads[0], grads[1], grads[2], grads[3], grads[4], grads[5], grads[6], grads[7], grads[8], grads[9], grads[10], grads[11], grads[12], grads[13], grads[14], grads[15], grads[16], grads[17], grads[18], grads[19])
```

```python
import functools

import jax
import jax.numpy as jnp
from jax import lax
from jax.experimental import pallas as pl
from jax.experimental.pallas import tpu as pltpu
from jax.sharding import PartitionSpec as P

HEADS = 8
KV_HEADS = 2
STATE = 128
SSM = 1536


HIGH_ACCURACY = lax.Precision.HIGHEST
EPSILON = 1e-05
ROPE_BASE = 100000000000.0
MASKED = -1e30


def passed_along(value, axis, steps):
    count = lax.axis_size(axis)
    first, last = (max(0, -steps), min(count, count - steps))
    return lax.ppermute(value, axis, [(source, source + steps) for source in range(first, last)])


def carried(payload, axis, backward, log_totals=None):
    count, mine = (lax.axis_size(axis), lax.axis_index(axis))
    pieces = lax.all_gather(payload, axis)
    if log_totals is None:
        log_totals = jnp.sum(pieces[:, :, STATE : STATE + 3].astype(jnp.float32), axis=2)
    place = jnp.arange(count, dtype=jnp.int32)
    if backward:
        between = (place[None, :] < place[:, None]) & (place[None, :] > mine)
        used = place > mine
    else:
        between = (place[None, :] > place[:, None]) & (place[None, :] < mine)
        used = place < mine
    decay = jnp.sum(jnp.where(between[:, :, None, None], log_totals[None], 0.0), axis=1)
    weight = jnp.where(used[:, None, None], jnp.exp(decay), 0.0)
    state = jnp.sum(weight[:, :, None, :] * pieces[:, :, :STATE].astype(jnp.float32), axis=0)
    return state, log_totals


def summed_share(value, axis):
    count = lax.axis_size(axis)
    pieces = value.astype(jnp.bfloat16).reshape(count, value.shape[0] // count, *value.shape[1:])
    landed = lax.all_to_all(pieces, axis, 0, 0)
    return jnp.sum(landed.astype(jnp.float32), axis=0)


def summed_rows(value, axis):
    count = lax.axis_size(axis)
    sequences, rows, width = value.shape
    pieces = value.astype(jnp.bfloat16).reshape(sequences, count, rows // count, width)
    landed = lax.all_to_all(pieces, axis, 1, 1)
    return jnp.sum(landed.astype(jnp.float32), axis=1)


def summed_everywhere(value, axis):
    share = summed_share(value, axis).astype(jnp.bfloat16)
    return lax.all_gather(share, axis, axis=0, tiled=True).astype(jnp.float32)


def matmul(left_operand, right_operand):
    return jnp.einsum(
        "std,de->ste", left_operand, right_operand, preferred_element_type=jnp.float32
    )


def matmul_back(grad, right_operand):
    return jnp.einsum("ste,de->std", grad, right_operand, preferred_element_type=jnp.float32)


def weight_grad(left_operand, grad):
    return jnp.einsum("std,ste->de", left_operand, grad, preferred_element_type=jnp.float32)


def rms_norm(values, gain):
    factor = lax.rsqrt(jnp.mean(values * values, axis=-1, keepdims=True) + EPSILON)
    return values * factor * gain


def rotate(values, positions):
    half = values.shape[-1] // 2
    freq = ROPE_BASE ** (-jnp.arange(half, dtype=jnp.float32) * 2.0 / values.shape[-1])
    angle = positions[:, None] * freq[None, :]
    cosine = jnp.cos(angle)[None, :, None, :]
    sine = jnp.sin(angle)[None, :, None, :]
    first = values[..., :half]
    second = values[..., half:]
    return jnp.concatenate(
        [first * cosine - second * sine, second * cosine + first * sine], axis=-1
    )


CHUNK = 128
LANES = 128
HALO = 8
VMEM_BYTES = 56 * 1024 * 1024


def dot(left, right, left_dim, right_dim):
    return lax.dot_general(
        left, right, (((left_dim,), (right_dim,)), ((), ())), preferred_element_type=jnp.float32
    )


def halves(value):
    high = value.astype(jnp.bfloat16)
    return high, (value - high.astype(jnp.float32)).astype(jnp.bfloat16)


def dot3(left, right, left_dim, right_dim):
    return (
        dot(left[0], right[0], left_dim, right_dim)
        + dot(left[0], right[1], left_dim, right_dim)
        + dot(left[1], right[0], left_dim, right_dim)
    )


def exact_dot(left, right, left_dim, right_dim):
    return lax.dot_general(
        left,
        right,
        (((left_dim,), (right_dim,)), ((), ())),
        preferred_element_type=jnp.float32,
        precision=HIGH_ACCURACY,
    )


def causal(block, columns):
    key_pos = lax.broadcasted_iota(jnp.int32, (block, columns), 0)
    query_pos = lax.rem(lax.broadcasted_iota(jnp.int32, (block, columns), 1), block)
    return key_pos <= query_pos


def attention_forward_kernel(block, query_ref, kv_ref, out_ref, log_ref, acc_ref):
    blocks_before = lax.axis_index("seq")
    queries = query_ref[0]
    columns = queries.shape[0]
    acc_ref[...] = jnp.zeros_like(acc_ref)

    def step(index, carry, masked):
        peak, total = carry
        keyvalue = kv_ref[0, pl.ds(pl.multiple_of(index * block, block), block), :]
        scores = dot(keyvalue, queries, 1, 1)
        if masked:
            scores = jnp.where(causal(block, columns), scores, MASKED)
        new_peak = jnp.maximum(peak, jnp.max(scores, axis=0, keepdims=True))
        probs = jnp.exp(scores - new_peak)
        scale = jnp.exp(peak - new_peak)
        acc_ref[...] = acc_ref[...] * scale + dot(keyvalue, probs.astype(jnp.bfloat16), 0, 0)
        return new_peak, total * scale + jnp.sum(probs, axis=0, keepdims=True)

    start = (jnp.full((1, columns), MASKED, jnp.float32), jnp.zeros((1, columns), jnp.float32))
    carry = lax.fori_loop(0, blocks_before, lambda i, c: step(i, c, False), start)
    peak, total = step(blocks_before, carry, True)
    log_ref[0] = peak + jnp.log(total)
    out_ref[0] = (acc_ref[...] / total).T


def attention_forward(block, queries, keyvalue):
    sequences, columns, width = queries.shape
    length = keyvalue.shape[1]
    per_sequence = lambda s: (s, 0, 0)
    return pl.pallas_call(
        functools.partial(attention_forward_kernel, block),
        grid=(sequences,),
        in_specs=[
            pl.BlockSpec((1, columns, width), per_sequence),
            pl.BlockSpec((1, length, width), per_sequence),
        ],
        out_specs=[
            pl.BlockSpec((1, columns, width), per_sequence),
            pl.BlockSpec((1, 1, columns), per_sequence),
        ],
        out_shape=[
            jax.ShapeDtypeStruct((sequences, columns, width), jnp.float32),
            jax.ShapeDtypeStruct((sequences, 1, columns), jnp.float32),
        ],
        scratch_shapes=[pltpu.VMEM((width, columns), jnp.float32)],
        compiler_params=pltpu.CompilerParams(vmem_limit_bytes=VMEM_BYTES),
        name="attention_forward",
    )(queries, keyvalue)


def attention_backward_kernel(
    block, query_ref, grad_ref, kv_ref, log_ref, delta_ref, query_grad_ref, kv_grad_ref, acc_ref
):
    blocks_before = lax.axis_index("seq")
    queries = query_ref[0]
    grads = grad_ref[0]
    columns = queries.shape[0]
    log_total = log_ref[0]
    delta = delta_ref[0]
    acc_ref[...] = jnp.zeros_like(acc_ref)
    blocks = kv_ref.shape[1] // block

    def step(index, masked):
        place = pl.ds(pl.multiple_of(index * block, block), block)
        keyvalue = kv_ref[0, place, :]
        scores = dot(keyvalue, queries, 1, 1)
        if masked:
            scores = jnp.where(causal(block, columns), scores, MASKED)
        probs = jnp.exp(scores - log_total)
        probs_grad = dot(keyvalue, grads, 1, 1)
        scores_grad = (probs * (probs_grad - delta)).astype(jnp.bfloat16)
        acc_ref[...] += dot(keyvalue, scores_grad, 0, 0)
        kv_grad = dot(scores_grad, queries, 1, 0) + dot(probs.astype(jnp.bfloat16), grads, 1, 0)
        kv_grad_ref[0, place, :] = kv_grad.astype(kv_grad_ref.dtype)

    @pl.loop(0, blocks_before)
    def _(index):
        step(index, False)

    step(blocks_before, True)

    @pl.loop(blocks_before + 1, blocks)
    def _(index):
        place = pl.ds(pl.multiple_of(index * block, block), block)
        kv_grad_ref[0, place, :] = jnp.zeros((block, kv_grad_ref.shape[2]), kv_grad_ref.dtype)

    query_grad_ref[0] = acc_ref[...].T


def attention_backward(block, queries, grads, keyvalue, log_total, delta):
    sequences, columns, width = queries.shape
    length = keyvalue.shape[1]
    per_sequence = lambda s: (s, 0, 0)
    wide = pl.BlockSpec((1, columns, width), per_sequence)
    line = pl.BlockSpec((1, 1, columns), per_sequence)
    whole = pl.BlockSpec((1, length, width), per_sequence)
    return pl.pallas_call(
        functools.partial(attention_backward_kernel, block),
        grid=(sequences,),
        in_specs=[wide, wide, whole, line, line],
        out_specs=[wide, whole],
        out_shape=[
            jax.ShapeDtypeStruct((sequences, columns, width), jnp.float32),
            jax.ShapeDtypeStruct((sequences, length, width), jnp.bfloat16),
        ],
        scratch_shapes=[pltpu.VMEM((width, columns), jnp.float32)],
        compiler_params=pltpu.CompilerParams(vmem_limit_bytes=VMEM_BYTES),
        name="attention_backward",
    )(queries, grads, keyvalue, log_total, delta)


def spreader(width, head_width):
    lane = lax.rem(lax.broadcasted_iota(jnp.int32, (2 * LANES, width), 0), LANES)
    owner = lax.broadcasted_iota(jnp.int32, (2 * LANES, width), 1) // head_width
    return (lane == owner).astype(jnp.bfloat16)


def spread(value, ones):
    return dot(jnp.concatenate(halves(value), axis=1), ones, 1, 0)


def gathered(value, ones):
    high, low = halves(value)
    one = ones[:LANES]
    return dot(high, one, 1, 1) + dot(low, one, 1, 1)


def triangle():
    row = lax.broadcasted_iota(jnp.int32, (CHUNK, CHUNK), 0)
    column = lax.broadcasted_iota(jnp.int32, (CHUNK, CHUNK), 1)
    return row, column


def conv_window(ext_ref, conv_ref, start, rows, taps):
    total = None
    for tap in range(taps):
        term = ext_ref[pl.ds(start + HALO - taps + 1 + tap, rows), :] * conv_ref[tap : tap + 1, :]
        total = term if total is None else total + term
    return total


def load_extended(inner_ref, state_ref, halo_ref, ext_ref):
    rows, width = inner_ref.shape[1], inner_ref.shape[2]
    ext_ref[0:HALO, :] = halo_ref[0]
    ext_ref[HALO : HALO + rows, 0:width] = inner_ref[0]
    ext_ref[HALO : HALO + rows, width:] = state_ref[0]


def step_sizes(raw, params_ref):
    shifted = raw + params_ref[0:1, :]
    step = jnp.maximum(shifted, 0.0) + jnp.log1p(jnp.exp(-jnp.abs(shifted)))
    return shifted, step, -step * params_ref[1:2, :]


def running_in_chunk(logdecay):
    row, column = triangle()
    lower = (row >= column).astype(jnp.float32)
    running = exact_dot(lower, logdecay, 1, 0)
    return running, running.T


def chunk_parts(ext_ref, conv_ref, raw_ref, params_ref, ones, start, width, taps, before=None):
    pre = conv_window(ext_ref, conv_ref, start, CHUNK, taps)
    sigma = jax.nn.sigmoid(pre)
    act = pre * sigma
    raw = raw_ref[0, pl.ds(start, CHUNK), :]
    shifted, step, logdecay = step_sizes(raw, params_ref)
    running, across = running_in_chunk(logdecay)
    last = running[CHUNK - 1 : CHUNK, :]
    channels = act[:, :width]
    writes = act[:, width : width + STATE]
    reads = act[:, width + STATE :]
    narrow = [step, jnp.exp(running), jnp.exp(last - running)]
    if before is not None:
        narrow.append(jnp.exp(running + before))
    wide = spread(jnp.concatenate(narrow, axis=0), ones)
    step_wide = wide[:CHUNK]
    grown = wide[CHUNK : 2 * CHUNK]
    tail = wide[2 * CHUNK : 3 * CHUNK]
    reach = wide[3 * CHUNK :]
    return dict(
        pre=pre, sigma=sigma, shifted=shifted, step=step, logdecay=logdecay, running=running,
        across=across, last=last, channels=channels, writes=writes, reads=reads,
        step_wide=step_wide, grown=grown, tail=tail, reach=reach,
        last_factor=grown[CHUNK - 1 : CHUNK],
        stepped=channels * step_wide,
    )


def decay_block(part, head, mask):
    spread_of = part["running"][:, head : head + 1] - part["across"][head : head + 1, :]
    return jnp.exp(jnp.where(mask, spread_of, MASKED))


def ssm_forward_kernel(
    heads, taps, inner_ref, state_ref, halo_ref, raw_ref, conv_ref, params_ref, skip_ref,
    y_ref, reach_ref, reads_ref, end_ref, ext_ref
):
    rows, width = inner_ref.shape[1], inner_ref.shape[2]
    head_width = width // heads
    load_extended(inner_ref, state_ref, halo_ref, ext_ref)
    ones = spreader(width, head_width)
    row, column = triangle()
    mask = row >= column
    state = jnp.zeros((STATE, width), jnp.float32)
    before = jnp.zeros((1, LANES), jnp.float32)
    for chunk in range(rows // CHUNK):
        start = chunk * CHUNK
        part = chunk_parts(
            ext_ref, conv_ref, raw_ref, params_ref, ones, start, width, taps, before
        )
        writes, reads = halves(part["writes"]), halves(part["reads"])
        meeting = dot3(reads, writes, 1, 1)
        stepped = part["stepped"]
        pieces = []
        for head in range(heads):
            mixing = halves(decay_block(part, head, mask) * meeting)
            own = halves(stepped[:, head * head_width : (head + 1) * head_width])
            pieces.append(dot3(mixing, own, 1, 0))
        y = jnp.concatenate(pieces, axis=1) + skip_ref[0:1, :] * part["channels"]
        if chunk:
            y = y + part["grown"] * dot3(reads, halves(state), 1, 0)
        y_ref[0, pl.ds(start, CHUNK), :] = y
        reach_ref[0, pl.ds(start, CHUNK), :] = part["reach"]
        reads_ref[0, pl.ds(start, CHUNK), :] = part["reads"]
        state = part["last_factor"] * state + dot3(writes, halves(stepped * part["tail"]), 0, 0)
        before = before + part["last"]
    end_ref[0, 0:STATE, :] = state.astype(jnp.bfloat16)
    rest = spread(jnp.broadcast_to(before, (8, LANES)), ones)[0:1]
    lines = []
    for _ in range(3):
        high = rest.astype(jnp.bfloat16).astype(jnp.float32)
        lines.append(high)
        rest = rest - high
    lines.append(jnp.zeros((HALO - 3, width), jnp.float32))
    lines.append(jnp.zeros((8, width), jnp.float32))
    end_ref[0, STATE:, :] = jnp.concatenate(lines, axis=0).astype(jnp.bfloat16)


def ssm_forward(heads, taps, inner, state, halo, raw, conv, params, skip):
    sequences, rows, width = inner.shape
    total = width + 2 * STATE
    each = lambda s: (s, 0, 0)
    same = lambda s: (0, 0)
    return pl.pallas_call(
        functools.partial(ssm_forward_kernel, heads, taps),
        grid=(sequences,),
        in_specs=[
            pl.BlockSpec((1, rows, width), each),
            pl.BlockSpec((1, rows, 2 * STATE), each),
            pl.BlockSpec((1, HALO, total), each),
            pl.BlockSpec((1, rows, LANES), each),
            pl.BlockSpec((8, total), same),
            pl.BlockSpec((8, LANES), same),
            pl.BlockSpec((8, width), same),
        ],
        out_specs=[
            pl.BlockSpec((1, rows, width), each),
            pl.BlockSpec((1, rows, width), each),
            pl.BlockSpec((1, rows, STATE), each),
            pl.BlockSpec((1, STATE + 16, width), each),
        ],
        out_shape=[
            jax.ShapeDtypeStruct((sequences, rows, width), jnp.float32),
            jax.ShapeDtypeStruct((sequences, rows, width), jnp.float32),
            jax.ShapeDtypeStruct((sequences, rows, STATE), jnp.float32),
            jax.ShapeDtypeStruct((sequences, STATE + 16, width), jnp.bfloat16),
        ],
        scratch_shapes=[pltpu.VMEM((HALO + rows, total), jnp.float32)],
        compiler_params=pltpu.CompilerParams(vmem_limit_bytes=VMEM_BYTES),
        name="ssm_forward",
    )(inner, state, halo, raw, conv, params, skip)


def ssm_backward_kernel(
    heads, taps, inner_ref, state_ref, halo_ref, raw_ref, conv_ref, params_ref, skip_ref,
    y_ref, y_grad_ref, start_ref, end_grad_ref,
    ext_grad_ref, raw_grad_ref, conv_grad_ref, small_ref, ext_ref, pre_grad_ref, kept_ref
):
    rows, width = inner_ref.shape[1], inner_ref.shape[2]
    head_width = width // heads
    load_extended(inner_ref, state_ref, halo_ref, ext_ref)
    ones = spreader(width, head_width)
    row, column = triangle()
    mask = row >= column
    upper = (row <= column).astype(jnp.float32)
    chunks = rows // CHUNK
    state = start_ref[0]
    parts = []
    for chunk in range(chunks):
        start = chunk * CHUNK
        kept_ref[chunk] = state
        if chunk < chunks - 1:
            part = chunk_parts(ext_ref, conv_ref, raw_ref, params_ref, ones, start, width, taps)
            state = part["last_factor"] * state + dot3(
                halves(part["writes"]), halves(part["stepped"] * part["tail"]), 0, 0
            )
    pre_grad_ref[0:HALO, :] = jnp.zeros((HALO, pre_grad_ref.shape[1]), jnp.float32)
    pre_grad_ref[HALO + rows :, :] = jnp.zeros((HALO, pre_grad_ref.shape[1]), jnp.float32)
    grad = end_grad_ref[0]
    skip = skip_ref[0:1, :]
    decay_sum = jnp.zeros((1, LANES), jnp.float32)
    bias_sum = jnp.zeros((1, LANES), jnp.float32)
    skip_sum = jnp.zeros((1, width), jnp.float32)
    for chunk in reversed(range(chunks)):
        start = chunk * CHUNK
        part = chunk_parts(ext_ref, conv_ref, raw_ref, params_ref, ones, start, width, taps)
        channels, stepped, grown = part["channels"], part["stepped"], part["grown"]
        writes, reads = halves(part["writes"]), halves(part["reads"])
        meeting = dot3(reads, writes, 1, 1)
        y_grad = y_grad_ref[0, pl.ds(start, CHUNK), :]
        y = y_ref[0, pl.ds(start, CHUNK), :]
        state = kept_ref[chunk]
        state_halves = halves(state)
        grad_halves = halves(grad)
        meeting_grad = jnp.zeros((CHUNK, CHUNK), jnp.float32)
        pieces = []
        for head in range(heads):
            own = slice(head * head_width, (head + 1) * head_width)
            decay = decay_block(part, head, mask)
            mixing = halves(decay * meeting)
            own_grad = halves(y_grad[:, own])
            pieces.append(dot3(mixing, own_grad, 0, 0))
            meeting_grad += dot3(own_grad, halves(stepped[:, own]), 1, 1) * decay
        tail_grad = part["tail"] * dot3(writes, grad_halves, 1, 0)
        pulled = jnp.concatenate(pieces, axis=1) + tail_grad
        channels_grad = part["step_wide"] * pulled + skip * y_grad
        reached = y_grad * grown
        reached_halves = halves(reached)
        meeting_halves = halves(meeting_grad)
        ended_halves = halves(stepped * part["tail"])
        writes_grad = dot3(meeting_halves, reads, 0, 0) + dot3(ended_halves, grad_halves, 1, 1)
        reads_grad = dot3(meeting_halves, writes, 1, 0) + dot3(reached_halves, state_halves, 1, 1)
        last_factor = part["last_factor"]
        last_terms = jnp.sum(stepped * tail_grad, axis=0, keepdims=True) + last_factor * jnp.sum(
            grad * state, axis=0, keepdims=True
        )
        sums = gathered(
            jnp.concatenate(
                [
                    y_grad * (y - skip * channels) - stepped * pulled,
                    channels * pulled,
                    jnp.broadcast_to(last_terms, (8, width)),
                ],
                axis=0,
            ),
            ones,
        )
        running_grad = sums[:CHUNK]
        step_grad = sums[CHUNK : 2 * CHUNK]
        logdecay_grad = exact_dot(upper, running_grad, 1, 0) + sums[2 * CHUNK : 2 * CHUNK + 1]
        step_grad = step_grad - logdecay_grad * params_ref[1:2, :]
        raw_grad = step_grad * jax.nn.sigmoid(part["shifted"])
        raw_grad_ref[0, pl.ds(start, CHUNK), :] = raw_grad
        bias_sum += jnp.sum(raw_grad, axis=0, keepdims=True)
        decay_sum += jnp.sum(logdecay_grad * part["logdecay"], axis=0, keepdims=True)
        skip_sum += jnp.sum(y_grad * channels, axis=0, keepdims=True)
        act_grad = jnp.concatenate([channels_grad, writes_grad, reads_grad], axis=1)
        sigma = part["sigma"]
        pre_grad_ref[pl.ds(HALO + start, CHUNK), :] = (
            act_grad * sigma * (1.0 + part["pre"] * (1.0 - sigma))
        )
        grad = last_factor * grad + dot3(reads, reached_halves, 0, 0)
    small_ref[0] = jnp.concatenate(
        [
            bias_sum,
            decay_sum,
            gathered(jnp.broadcast_to(skip_sum, (8, width)), ones)[0:1],
            jnp.zeros((5, LANES), jnp.float32),
        ],
        axis=0,
    )
    count = HALO + rows
    total = None
    for tap in range(taps):
        term = pre_grad_ref[pl.ds(taps - 1 - tap, count), :] * conv_ref[tap : tap + 1, :]
        total = term if total is None else total + term
    ext_grad_ref[0] = total
    pre_grad = pre_grad_ref[pl.ds(HALO, rows), :]
    lines = [
        jnp.sum(
            pre_grad * ext_ref[pl.ds(HALO - taps + 1 + tap, rows), :], axis=0, keepdims=True
        )
        for tap in range(taps)
    ]
    lines.append(jnp.zeros((8 - taps, total.shape[1]), jnp.float32))
    conv_grad_ref[0] = jnp.concatenate(lines, axis=0)


def ssm_backward(heads, taps, inner, state, halo, raw, conv, params, skip, y, y_grad, begin, end_grad):
    sequences, rows, width = inner.shape
    total = width + 2 * STATE
    each = lambda s: (s, 0, 0)
    same = lambda s: (0, 0)
    return pl.pallas_call(
        functools.partial(ssm_backward_kernel, heads, taps),
        grid=(sequences,),
        in_specs=[
            pl.BlockSpec((1, rows, width), each),
            pl.BlockSpec((1, rows, 2 * STATE), each),
            pl.BlockSpec((1, HALO, total), each),
            pl.BlockSpec((1, rows, LANES), each),
            pl.BlockSpec((8, total), same),
            pl.BlockSpec((8, LANES), same),
            pl.BlockSpec((8, width), same),
            pl.BlockSpec((1, rows, width), each),
            pl.BlockSpec((1, rows, width), each),
            pl.BlockSpec((1, STATE, width), each),
            pl.BlockSpec((1, STATE, width), each),
        ],
        out_specs=[
            pl.BlockSpec((1, HALO + rows, total), each),
            pl.BlockSpec((1, rows, LANES), each),
            pl.BlockSpec((1, 8, total), each),
            pl.BlockSpec((1, 8, LANES), each),
        ],
        out_shape=[
            jax.ShapeDtypeStruct((sequences, HALO + rows, total), jnp.float32),
            jax.ShapeDtypeStruct((sequences, rows, LANES), jnp.float32),
            jax.ShapeDtypeStruct((sequences, 8, total), jnp.float32),
            jax.ShapeDtypeStruct((sequences, 8, LANES), jnp.float32),
        ],
        scratch_shapes=[
            pltpu.VMEM((HALO + rows, total), jnp.float32),
            pltpu.VMEM((2 * HALO + rows, total), jnp.float32),
            pltpu.VMEM((rows // CHUNK, STATE, width), jnp.float32),
        ],
        compiler_params=pltpu.CompilerParams(vmem_limit_bytes=VMEM_BYTES),
        name="ssm_backward",
    )(inner, state, halo, raw, conv, params, skip, y, y_grad, begin, end_grad)


def on_device(
    hidden_in,
    norm_gain,
    query_weight,
    keyvalue_matrix,
    output_weight,
    zgate_weight,
    inner_weight,
    state_weight,
    step_weight,
    conv_inner,
    conv_state,
    step_bias,
    decay_log,
    skip_gain,
    ssm_gain,
    mixer_weight,
    mlp_gain,
    gate_weight,
    up_weight,
    down_weight,
    grad_output,
):
    sequences, rows, width = hidden_in.shape
    head_dim = keyvalue_matrix.shape[2] // 2
    heads_here = query_weight.shape[1] // head_dim
    group = HEADS // KV_HEADS
    factor = head_dim ** (-0.5)
    inner_width = inner_weight.shape[1]
    mamba_here = step_bias.shape[0]
    seq_index = lax.axis_index("seq")
    head_index = lax.axis_index("head")
    query_pos = seq_index * rows + jnp.arange(rows, dtype=jnp.int32)
    positions = query_pos.astype(jnp.float32)
    input_float = hidden_in.astype(jnp.float32)
    gain_one = norm_gain.astype(jnp.float32)
    normalized_input = rms_norm(input_float, gain_one).astype(jnp.bfloat16)
    query_raw = matmul(normalized_input, query_weight).reshape(
        sequences, rows, heads_here, head_dim
    )
    queries = rotate(query_raw, positions).astype(jnp.bfloat16)
    kv_index = head_index * heads_here // group
    own_weight = lax.dynamic_index_in_dim(keyvalue_matrix, kv_index, 1, keepdims=False)
    keyvalue_projected = matmul(normalized_input, own_weight)
    keys_own = rotate(keyvalue_projected[:, :, None, :head_dim], positions)[:, :, 0]
    keyvalue_own = jnp.concatenate([keys_own, keyvalue_projected[..., head_dim:]], axis=-1).astype(
        jnp.bfloat16
    )
    keyvalue_all = lax.all_gather(keyvalue_own, "seq", axis=1, tiled=True)

    def by_head(value, zeros_first):
        moved = value.transpose(0, 2, 1, 3).reshape(sequences, heads_here * rows, head_dim)
        zeros = jnp.zeros_like(moved)
        return jnp.concatenate([zeros, moved] if zeros_first else [moved, zeros], axis=-1)

    def by_token(value):
        moved = value.reshape(sequences, heads_here, rows, head_dim).transpose(0, 2, 1, 3)
        return moved.reshape(sequences, rows, heads_here * head_dim)

    queries_padded = by_head(queries * jnp.asarray(factor, jnp.bfloat16), False)
    zgate = matmul(normalized_input, zgate_weight)
    inner = matmul(normalized_input, inner_weight)
    state_inner = matmul(normalized_input, state_weight)
    step_raw = matmul(normalized_input, jnp.pad(step_weight, ((0, 0), (0, LANES - mamba_here))))
    conv_weight = jnp.concatenate([conv_inner, conv_state], axis=1).astype(jnp.float32)
    taps = conv_weight.shape[0]
    conv_padded = jnp.pad(conv_weight, ((0, 8 - taps), (0, 0)))
    ends = jnp.concatenate([inner[:, rows - HALO :], state_inner[:, rows - HALO :]], axis=-1)
    halo = passed_along(ends, "seq", 1)
    lane_pad = (0, LANES - mamba_here)
    step_params = jnp.pad(
        jnp.stack([step_bias, jnp.exp(decay_log)]), ((0, 6), lane_pad)
    )
    skip_wide = jnp.broadcast_to(
        jnp.repeat(skip_gain, inner_width // mamba_here)[None], (8, inner_width)
    )
    y_local, reach, reads, state_payload = ssm_forward(
        mamba_here, taps, inner, state_inner, halo, step_raw, conv_padded, step_params, skip_wide
    )
    attended_wide, log_total = attention_forward(rows, queries_padded, keyvalue_all)
    attended = by_token(attended_wide[..., head_dim:].astype(jnp.bfloat16))
    state_in, log_totals = carried(state_payload, "seq", False)
    y_flat = y_local + reach * jnp.einsum(
        "stn,snw->stw", reads, state_in, precision=HIGH_ACCURACY
    )
    gated = y_flat * jax.nn.silu(zgate)
    squares = lax.psum(jnp.sum(gated * gated, axis=-1), "head")
    ssm_factor = lax.rsqrt(squares / SSM + EPSILON)[..., None]
    gain_ssm = ssm_gain.astype(jnp.float32)
    ssm_normed = (gated * ssm_factor * gain_ssm).astype(jnp.bfloat16)
    branch_part = matmul(attended, output_weight) + matmul(ssm_normed, mixer_weight)
    quarter = rows // lax.axis_size("head")
    mixed_rows = summed_rows(branch_part, "head")
    def own_rows(value):
        return lax.dynamic_slice_in_dim(value, head_index * quarter, quarter, 1)

    input_rows = own_rows(input_float)
    hidden_rows = input_rows + mixed_rows
    gain_two = mlp_gain.astype(jnp.float32)
    normed_two_rows = rms_norm(hidden_rows, gain_two).astype(jnp.bfloat16)
    normed_two = lax.all_gather(normed_two_rows, "head", axis=1, tiled=True)
    gate = matmul(normed_two, gate_weight)
    up = matmul(normed_two, up_weight)
    activated = (jax.nn.silu(gate) * up).astype(jnp.bfloat16)
    feed_part = matmul(activated, down_weight)
    feed_own = summed_rows(feed_part, "head")
    output_own = (hidden_rows + feed_own).astype(jnp.bfloat16)
    output = lax.all_gather(output_own, "head", axis=1, tiled=True)
    act_grad = matmul_back(grad_output, down_weight)
    grad_down = weight_grad(activated, grad_output)
    gate_pull = jax.vjp(lambda gate_in, up_in: jax.nn.silu(gate_in) * up_in, gate, up)[1]
    gate_grad, up_grad = gate_pull(act_grad)
    gate_grad = gate_grad.astype(jnp.bfloat16)
    up_grad = up_grad.astype(jnp.bfloat16)
    grad_gate = weight_grad(normed_two, gate_grad)
    grad_up = weight_grad(normed_two, up_grad)
    normed_two_grad = summed_rows(
        matmul_back(gate_grad, gate_weight) + matmul_back(up_grad, up_weight), "head"
    )
    units = grad_down.shape[0]
    down_sum = summed_everywhere(grad_down, "seq")
    feed_sums = summed_everywhere(jnp.concatenate([grad_gate, grad_up], axis=1), "seq")
    norm_two_pull = jax.vjp(rms_norm, hidden_rows, gain_two)[1]
    hidden_norm_grad, grad_gain_two = norm_two_pull(normed_two_grad)
    hidden_grad = own_rows(grad_output).astype(jnp.float32) + hidden_norm_grad
    mixed_grad = lax.all_gather(
        hidden_grad.astype(jnp.bfloat16), "head", axis=1, tiled=True
    )
    grad_output_proj = weight_grad(attended, mixed_grad)
    attended_grad = matmul_back(mixed_grad, output_weight).astype(jnp.bfloat16)
    grads_padded = by_head(attended_grad.reshape(sequences, rows, heads_here, head_dim), True)
    delta = jnp.sum(grads_padded.astype(jnp.float32) * attended_wide, axis=-1)[:, None, :]
    grad_mixer = weight_grad(ssm_normed, mixed_grad)
    mixed_sums = summed_everywhere(jnp.concatenate([grad_output_proj, grad_mixer], axis=0), "seq")
    ssm_normed_grad = matmul_back(mixed_grad, mixer_weight)
    weighted = ssm_normed_grad * gain_ssm
    inner_total = lax.psum(jnp.sum(weighted * gated, axis=-1), "head")
    gated_grad = weighted * ssm_factor - gated * ssm_factor**3 * inner_total[..., None] / SSM
    grad_gain_ssm = jnp.sum(ssm_normed_grad * gated * ssm_factor, axis=(0, 1))
    gated_pull = jax.vjp(lambda y_in, z_in: y_in * jax.nn.silu(z_in), y_flat, zgate)[1]
    y_grad, zgate_grad = gated_pull(gated_grad)
    zgate_grad = zgate_grad.astype(jnp.bfloat16)
    grad_zgate = weight_grad(normalized_input, zgate_grad)
    own_state_grad = jnp.einsum(
        "stn,stw->snw", reads, reach * y_grad, precision=HIGH_ACCURACY
    )
    state_grad, _ = carried(own_state_grad.astype(jnp.bfloat16), "seq", True, log_totals)
    extended_grad, raw_grad, conv_grad, small_grad = ssm_backward(
        mamba_here, taps, inner, state_inner, halo, step_raw, conv_padded, step_params,
        skip_wide, y_flat, y_grad, state_in, state_grad,
    )
    step_raw_grad = raw_grad[..., :mamba_here]
    conv_grad = jnp.sum(conv_grad, axis=0)[:taps]
    small_grad = jnp.sum(small_grad, axis=0)[:, :mamba_here]
    grad_step_bias, grad_decay_log, grad_skip = small_grad[0], small_grad[1], small_grad[2]
    before_grad = passed_along(extended_grad[:, :HALO], "seq", -1)
    inner_grad = extended_grad[:, HALO:] + jnp.pad(before_grad, ((0, 0), (rows - HALO, 0), (0, 0)))
    inner_own = inner_grad[..., :inner_width].astype(jnp.bfloat16)
    step_grad = step_raw_grad.astype(jnp.bfloat16)
    grad_inner = weight_grad(normalized_input, inner_own)
    grad_step = weight_grad(normalized_input, step_grad)
    query_grad, keyvalue_grad_all = attention_backward(
        rows, queries_padded, grads_padded, keyvalue_all, log_total, delta
    )
    query_grad = by_token(query_grad[..., :head_dim]).reshape(
        sequences, rows, heads_here, head_dim
    ) * factor
    keyvalue_grad_own = summed_rows(keyvalue_grad_all, "seq")
    key_raw_grad = rotate(keyvalue_grad_own[:, :, None, :head_dim], -positions)[:, :, 0]
    keyvalue_raw_grad = jnp.concatenate([key_raw_grad, keyvalue_grad_own[..., head_dim:]], axis=-1)
    chooser = (jnp.arange(KV_HEADS, dtype=jnp.int32) == kv_index).astype(jnp.float32)
    keyvalue_both = chooser[None, None, :, None] * keyvalue_raw_grad[:, :, None, :]
    query_raw_grad = (
        rotate(query_grad, -positions)
        .astype(jnp.bfloat16)
        .reshape(sequences, rows, heads_here * head_dim)
    )
    grad_query = weight_grad(normalized_input, query_raw_grad)
    normed_part = (
        matmul_back(query_raw_grad, query_weight)
        + matmul_back(zgate_grad, zgate_weight)
        + matmul_back(inner_own, inner_weight)
        + matmul_back(step_grad, step_weight)
    )
    kv_width = keyvalue_both.shape[2] * keyvalue_both.shape[3]
    together = summed_rows(
        jnp.concatenate(
            [
                normed_part,
                keyvalue_both.reshape(sequences, rows, kv_width),
                inner_grad[..., inner_width:],
            ],
            axis=-1,
        ),
        "head",
    )
    normed_sum = together[..., :width]
    low_rows = together[..., width:].astype(jnp.bfloat16)
    shared_weight = jnp.concatenate(
        [keyvalue_matrix.reshape(width, kv_width), state_weight], axis=1
    )
    grad_shared = weight_grad(own_rows(normalized_input), low_rows)
    normed_grad = normed_sum + matmul_back(low_rows, shared_weight)
    norm_one_pull = jax.vjp(rms_norm, input_rows, gain_one)[1]
    input_norm_grad, grad_gain_one = norm_one_pull(normed_grad)
    input_rows_grad = (hidden_grad + input_norm_grad).astype(jnp.bfloat16)
    grad_input = lax.all_gather(input_rows_grad, "head", axis=1, tiled=True).astype(jnp.float32)
    own_small = [
        grad_step,
        conv_grad[:, :inner_width],
        grad_step_bias,
        grad_decay_log,
        grad_skip,
        grad_gain_ssm,
    ]
    all_small = [grad_gain_one, grad_gain_two, conv_grad[:, inner_width:]]
    all_flat = lax.psum(jnp.concatenate([part.reshape(-1) for part in all_small]), "head")
    flat = jnp.concatenate([part.reshape(-1) for part in own_small] + [all_flat])
    extra = -(-flat.shape[0] // width // LANES) * LANES
    flat = jnp.pad(flat, (0, extra * width - flat.shape[0])).reshape(width, extra)
    last_sums = summed_everywhere(
        jnp.concatenate([grad_zgate, grad_inner, grad_query, flat], axis=1), "seq"
    )
    small_sums = last_sums[:, last_sums.shape[1] - extra :].reshape(-1)
    shared_part = summed_share(summed_share(grad_shared, "head"), "seq").astype(jnp.bfloat16)
    shared_sum = lax.all_gather(
        shared_part, ("head", "seq"), axis=0, tiled=True
    ).astype(jnp.float32)
    def unpacked(flat, likes):
        found, at = [], 0
        for like in likes:
            found.append(flat[at : at + like.size].reshape(like.shape))
            at += like.size
        return found

    (
        grad_step,
        conv_inner_grad,
        grad_step_bias,
        grad_decay_log,
        grad_skip,
        grad_gain_ssm,
        grad_gain_one,
        grad_gain_two,
        conv_state_grad,
    ) = unpacked(small_sums, own_small + all_small)
    attended_width = heads_here * head_dim
    return (
        output,
        grad_input,
        grad_gain_one,
        last_sums[:, 2 * inner_width : last_sums.shape[1] - extra],
        shared_sum[:, :kv_width].reshape(keyvalue_matrix.shape),
        mixed_sums[:attended_width],
        last_sums[:, :inner_width],
        last_sums[:, inner_width : 2 * inner_width],
        shared_sum[:, kv_width:],
        grad_step,
        conv_inner_grad,
        conv_state_grad,
        grad_step_bias,
        grad_decay_log,
        grad_skip,
        grad_gain_ssm,
        mixed_sums[attended_width:],
        grad_gain_two,
        feed_sums[:, :units],
        feed_sums[:, units:],
        down_sum,
    )


def solution(mesh):
    placed = (
        P(None, "seq", None),
        P(),
        P(None, "head"),
        P(),
        P("head", None),
        P(None, "head"),
        P(None, "head"),
        P(),
        P(None, "head"),
        P(None, "head"),
        P(),
        P("head"),
        P("head"),
        P("head"),
        P("head"),
        P("head", None),
        P(),
        P(None, "head"),
        P(None, "head"),
        P("head", None),
        P(None, "seq", None),
    )
    return jax.shard_map(
        on_device,
        mesh=mesh,
        in_specs=placed,
        out_specs=(
            P(None, "seq", None),
            P(None, "seq", None),
            P(),
            P(None, "head"),
            P(),
            P("head", None),
            P(None, "head"),
            P(None, "head"),
            P(),
            P(None, "head"),
            P(None, "head"),
            P(),
            P("head"),
            P("head"),
            P("head"),
            P("head"),
            P("head", None),
            P(),
            P(None, "head"),
            P(None, "head"),
            P("head", None),
        ),
        check_vma=False,
    )
```
